32 devices in a mesh: group: 2 (over x), lat: 16 (over z, y, core).
Axes of the slice: x: 2, y: 2, z: 4, core: 2. Of those that a mesh axis runs over, the one named last changes fastest.
Arguments:
- fields: bfloat16 [128, 40, 64, 128], P(('group', 'lat')), parts along dimension 0, may hold values from -6 to 6
- helm_coef: float32 [64, 5120], P('lat'), may hold values from 0.1 to 2
- weight_table: bfloat16 [64, 128, 128], replicated, may hold values from -0.1875 to 0.1875
- fetch_list: int32 [32, 7, 64], P(('group', 'lat')), parts along dimension 0, may hold values from 0 to 159, as said below
- source_owner: int32 [128, 40, 8], P(('group', 'lat')), parts along dimension 0, may hold values from 0 to 15, as said below
- source_slot: int32 [128, 40, 8], P(('group', 'lat')), parts along dimension 0, may hold values from 0 to 63
- weight_index: int32 [128, 40, 8], P(('group', 'lat')), parts along dimension 0, may hold values from 0 to 63
Outputs:
- adjusted: float32 [128, 4, 16, 5120], P(('group', 'lat')), parts along dimension 0
The draws below stay inside these ranges and needn't reach their ends.
There are 2 independent parts, one for each index of `group`. The reference program is written for one: setup_inputs(seed, part) draws one part's arguments, and reference() takes and returns one part's arrays. A program takes and returns all parts, laid end to end along the dimension named above; an argument that names none is the same for every part. Nothing has to cross between parts.
Inputs may be any that keep to these rules, and one draw needn't show every extreme that they name: `fetch_list`: the 64 numbers of one list are distinct. `source_owner`: the band of a source differs from the band of its arrival row by at most 3.
All inputs are finite; a program needn't handle non-finite values.
Results may differ from the reference program's by a relative error of at most 0.0003.
Values may be sent and summed in bfloat16 or wider, within the bound.
A program may use at most 128 MiB of HBM per device.

```python
import math
import jax
import jax.numpy as jnp
from jax import lax

NLON = 5120
BW = 128
FLD = 4
LEV = 16
TAPS = 8
REACH = 3
CAP = 64
WTAB = 64
SWEEPS = 2
ROWS_DEV = 4
NB = 40
NLAT = 64
N_LAT = 16


def route_tables(key):
    blocks_band = ROWS_DEV * NB
    offsets = 2 * REACH + 1
    key_list, key_far, key_near, key_wide, key_slot = jax.random.split(key, 5)
    list_keys = jax.random.split(key_list, N_LAT * offsets)
    lists = jax.vmap(lambda one_key: jax.random.permutation(one_key, blocks_band)[:CAP])(list_keys)
    lists = lists.reshape(N_LAT, offsets, CAP).astype(jnp.int32)
    shape = (N_LAT, blocks_band, TAPS)
    bands = jnp.broadcast_to(jnp.arange(N_LAT, dtype=jnp.int32)[:, None, None], shape)
    polar = jnp.abs(2 * bands - (N_LAT - 1))
    distant = jax.random.randint(key_far, shape, 0, N_LAT) < polar
    nearby = jax.random.randint(key_near, shape, -1, 2)
    spread = jax.random.randint(key_wide, shape, -REACH, REACH + 1)
    moved = jnp.where(distant, spread, nearby)
    owners = bands + moved
    owners = jnp.where((owners < 0) | (owners >= N_LAT), bands - moved, owners)
    slots = jax.random.randint(key_slot, shape, 0, CAP)
    return (lists, owners.reshape(NLAT, NB, TAPS).astype(jnp.int32), slots.reshape(NLAT, NB, TAPS).astype(jnp.int32))


def draw_fetch_list(key, part):
    tables = route_tables(key)
    return tables[0]


def draw_source_owner(key, part):
    tables = route_tables(key)
    return tables[1]


def draw_source_slot(key, part):
    tables = route_tables(key)
    return tables[2]


def plant(drawn, stream_key, smallest, top_value):
    dims = drawn.shape
    place = [jax.random.randint(jax.random.fold_in(stream_key, axis), (), 0, dims[axis]) for axis in range(len(dims))]
    drawn = drawn.at[tuple(place)].set(smallest)
    longest = dims.index(max(dims))
    place[longest] = (place[longest] + 1) % dims[longest]
    return drawn.at[tuple(place)].set(top_value)


def level_of(own_key, dims, cuts, smallest, high):
    loudness = 1.0
    for axis_at, shards_of in cuts:
        steps = jax.random.uniform(jax.random.fold_in(jax.random.fold_in(own_key, 6), axis_at), (shards_of,), jnp.float32, smallest / len(cuts), high / len(cuts))
        loudness = loudness * jnp.repeat(jnp.exp(steps), dims[axis_at] // shards_of).reshape((-1,) + (1,) * (len(dims) - 1 - axis_at))
    return loudness


def centred(own_key, shape, deviation, bound, pieces=(), held_as=jnp.bfloat16):
    entries = deviation * jax.random.normal(own_key, shape, jnp.float32)
    if pieces:
        entries = entries * level_of(own_key, shape, pieces, -0.22, 0.18)
    return jnp.clip(entries, -bound, bound).astype(held_as)


def setup_inputs(seed: int = 0, part: int = 0) -> dict:
    seeds = jax.random.split(jax.random.key(seed), 8)
    part_keys = jax.random.split(jax.random.fold_in(seeds[7], part), 8)
    fields = centred(part_keys[0], (NLAT, NB, FLD * LEV, BW), 1.0, 6.0, ((0, 16),))
    helm_coef = jnp.clip(jnp.exp(math.log(2.0) - 2.9957323 * jax.random.uniform(seeds[1], (NLAT, NLON), jnp.float32) ** level_of(seeds[1], (NLAT, NLON), ((0, 16),), -0.2, 0.2)), 0.1, 2.0)
    weight_table = centred(seeds[2], (WTAB, BW, BW), (TAPS * BW) ** -0.5, 0.1875)
    fetch_list = draw_fetch_list(jax.random.fold_in(jax.random.fold_in(seeds[7], part), 71), part)
    source_owner = draw_source_owner(jax.random.fold_in(jax.random.fold_in(seeds[7], part), 71), part)
    source_slot = draw_source_slot(jax.random.fold_in(jax.random.fold_in(seeds[7], part), 71), part)
    weight_index = plant(jax.random.randint(part_keys[6], (NLAT, NB, TAPS), 0, WTAB), jax.random.fold_in(part_keys[6], 1), 0, WTAB - 1).astype(jnp.int32)
    return {"fields": fields, "helm_coef": helm_coef, "weight_table": weight_table, "fetch_list": fetch_list, "source_owner": source_owner, "source_slot": source_slot, "weight_index": weight_index}


lon_coupling = 0.25
lat_coupling = 1.0
lev_coupling = 0.25


def couple(field, north_south):
    east_west = jnp.roll(field, 1, axis=3) + jnp.roll(field, -1, axis=3)
    padded = jnp.pad(field, ((0, 0), (0, 0), (1, 1), (0, 0)))
    vertical = padded[:, :, 2:] + padded[:, :, :-2]
    return lon_coupling * east_west + lat_coupling * north_south + lev_coupling * vertical


def reference(fields, helm_coef, weight_table, fetch_list, source_owner, source_slot, weight_index):
    blocks_band = ROWS_DEV * NB
    planes = FLD * LEV
    bands = (jnp.arange(NLAT, dtype=jnp.int32) // ROWS_DEV)[:, None, None]
    bands = jnp.broadcast_to(bands, source_owner.shape)
    local_ids = fetch_list[bands, source_owner - bands + REACH, source_slot]
    global_ids = (source_owner * blocks_band + local_ids).astype(jnp.int32)
    flat = fields.reshape(NLAT * NB, planes, BW)

    def one_row(inputs):
        row_ids, row_weights = inputs
        sources = jnp.take(flat, row_ids, axis=0).astype(jnp.float32)
        weights = jnp.take(weight_table, row_weights, axis=0).astype(jnp.float32)
        return jnp.einsum("nrpy,nryx->npx", sources, weights)

    departed = lax.map(one_row, (global_ids, weight_index))
    departed = departed.transpose(0, 2, 1, 3).reshape(NLAT, FLD, LEV, NB * BW)
    diagonal = helm_coef[:, None, None, :] + 2.0 * (lon_coupling + lat_coupling + lev_coupling)
    field = departed / diagonal
    for sweep in range(SWEEPS):
        padded = jnp.pad(field, ((1, 1), (0, 0), (0, 0), (0, 0)))
        field = (departed + couple(field, padded[2:] + padded[:-2])) / diagonal
    return field
```

```python
import functools

import jax
import jax.numpy as jnp
from jax import lax
from jax.experimental import pallas as pl
from jax.experimental.pallas import tpu as pltpu
from jax.sharding import PartitionSpec as P

FLD = 4
LEV = 16
SWEEPS = 2

lon_coupling = 0.25
lat_coupling = 1.0
lev_coupling = 0.25

MESH = pl.DeviceIdType.MESH


def relax_kernel(
    reach,
    bands,
    fields_ref,
    lists_smem,
    lists_vmem,
    helm_ref,
    table_hbm,
    pool_index_hbm,
    weight_index_hbm,
    out_hbm,
    table,
    pool_index,
    weight_index,
    asked_vmem,
    asked,
    packed,
    pool,
    inverse,
    departed,
    first,
    second,
    local_sem,
    list_send,
    list_recv,
    asked_sem,
    block_send,
    block_recv,
    halo_send,
    halo_recv,
    out_sem,
):
    me = lax.axis_index("lat")
    offsets, cap = lists_smem.shape
    rows, planes, lon = departed.shape
    width = fields_ref.shape[2]
    nblocks = lon // width
    taps = pool_index.shape[2]
    others = [r for r in range(offsets) if r != reach]
    others.sort(key=lambda r: -abs(r - reach))

    def there(step):
        band = me + (step - reach)
        return (band >= 0) & (band < bands)

    barrier = pltpu.get_barrier_semaphore()
    count = jnp.int32(0)
    for r in others:

        @pl.when(there(r))
        def _():
            pl.semaphore_signal(barrier, inc=1, device_id={"lat": me + (r - reach)}, device_id_type=MESH)

        count = count + there(r).astype(jnp.int32)
    pl.semaphore_wait(barrier, count)

    def list_copy(r):
        back = 2 * reach - r
        return pltpu.make_async_remote_copy(
            src_ref=lists_vmem,
            dst_ref=asked_vmem.at[back],
            send_sem=list_send.at[r],
            recv_sem=list_recv.at[back],
            device_id={"lat": me + (r - reach)},
            device_id_type=MESH,
        )

    for r in others:

        @pl.when(there(r))
        def _():
            list_copy(r).start()

    locals_ = [
        pltpu.make_async_copy(table_hbm, table, local_sem.at[0]),
        pltpu.make_async_copy(pool_index_hbm, pool_index, local_sem.at[1]),
        pltpu.make_async_copy(weight_index_hbm, weight_index, local_sem.at[2]),
    ]
    for copy in locals_:
        copy.start()

    def asked_copy(r):
        return pltpu.make_async_copy(asked_vmem.at[r], asked.at[r], asked_sem.at[r])

    for r in others:

        @pl.when(there(r))
        def _():
            list_copy(2 * reach - r).wait_recv()
            asked_copy(r).start()

    def block_copy(r):
        back = 2 * reach - r
        return pltpu.make_async_remote_copy(
            src_ref=packed.at[r],
            dst_ref=pool.at[pl.ds(back * cap, cap)],
            send_sem=block_send.at[r],
            recv_sem=block_recv.at[back],
            device_id={"lat": me + (r - reach)},
            device_id_type=MESH,
        )

    unroll = 8 if cap % 8 == 0 else 1
    for r in others:

        @pl.when(there(r))
        def _():
            asked_copy(r).wait()

            def pack(j, carry):
                for u in range(unroll):
                    packed[r, j * unroll + u] = fields_ref[asked[r, 2 * reach - r, j * unroll + u]]
                return carry

            lax.fori_loop(0, cap // unroll, pack, 0)
            block_copy(r).start()

    def pack_own(j, carry):
        for u in range(unroll):
            pool[reach * cap + j * unroll + u] = fields_ref[lists_smem[reach, j * unroll + u]]
        return carry

    lax.fori_loop(0, cap // unroll, pack_own, 0)

    total_coupling = 2.0 * (lon_coupling + lat_coupling + lev_coupling)
    inverse[...] = 1.0 / (helm_ref[...] + total_coupling)

    @pl.when(me == 0)
    def _():
        first[0] = jnp.zeros((planes, lon), jnp.float32)
        second[0] = jnp.zeros((planes, lon), jnp.float32)

    @pl.when(me == bands - 1)
    def _():
        first[rows + 1] = jnp.zeros((planes, lon), jnp.float32)
        second[rows + 1] = jnp.zeros((planes, lon), jnp.float32)

    for copy in locals_:
        copy.wait()
    for r in others:

        @pl.when(there(r))
        def _():
            block_copy(2 * reach - r).wait_recv()

    north, south = me > 0, me < bands - 1

    def halo_copy(sweep, way, f):
        held = (first, second)[sweep]
        planes_f = pl.ds(pl.multiple_of(f * LEV, LEV), LEV)
        return pltpu.make_async_remote_copy(
            src_ref=held.at[1 if way == 0 else rows, planes_f],
            dst_ref=held.at[rows + 1 if way == 0 else 0, planes_f],
            send_sem=halo_send.at[sweep, way, f],
            recv_sem=halo_recv.at[sweep, way, f],
            device_id={"lat": me - 1 if way == 0 else me + 1},
            device_id_type=MESH,
        )

    def interpolate(row):
        def one_block(b, carry):
            columns = pl.ds(pl.multiple_of(b * width, width), width)
            sources = jnp.concatenate([pool[pool_index[row, b, t]] for t in range(taps)], axis=1)
            weights = jnp.concatenate([table[weight_index[row, b, t]] for t in range(taps)], axis=0)
            value = jnp.dot(sources, weights, preferred_element_type=jnp.float32)
            departed[row, :, columns] = value
            first[row + 1, :, columns] = value * inverse[row : row + 1, columns]
            return carry

        lax.fori_loop(0, nblocks, one_block, 0)

    order = [0, rows - 1] + list(range(1, rows - 1))
    for row in order:
        interpolate(row)
        if row == 0:

            @pl.when(north)
            def _():
                for f in range(FLD):
                    halo_copy(0, 0, f).start()

        if row == rows - 1:

            @pl.when(south)
            def _():
                for f in range(FLD):
                    halo_copy(0, 1, f).start()

    chunk = 1024 if lon % 1024 == 0 else width
    lane = 128

    def relax(held, result, row, f):
        planes_f = pl.ds(pl.multiple_of(f * LEV, LEV), LEV)
        for start in range(0, lon, chunk):
            here = pl.ds(start, chunk)
            mid = held[row + 1, planes_f, here]
            west = held[row + 1, planes_f, pl.ds((start - lane) % lon, lane)]
            east = held[row + 1, planes_f, pl.ds((start + chunk) % lon, lane)]
            wide = jnp.concatenate([west, mid, east], axis=1)
            span = chunk + 2 * lane
            beside = pltpu.roll(wide, 1, 1) + pltpu.roll(wide, span - 1, 1)
            beside = beside[:, lane : lane + chunk]
            level = lax.broadcasted_iota(jnp.int32, (LEV, chunk), 0)
            above = jnp.where(level > 0, pltpu.roll(mid, 1, 0), 0.0)
            below = jnp.where(level < LEV - 1, pltpu.roll(mid, LEV - 1, 0), 0.0)
            across = held[row, planes_f, here] + held[row + 2, planes_f, here]
            coupled = lon_coupling * beside + lat_coupling * across + lev_coupling * (above + below)
            value = (departed[row, planes_f, here] + coupled) * inverse[row : row + 1, here]
            if result is departed:
                result[row, planes_f, here] = value
            else:
                result[row + 1, planes_f, here] = value

    def out_copy(row, f):
        planes_f = pl.ds(pl.multiple_of(f * LEV, LEV), LEV)
        return pltpu.make_async_copy(departed.at[row, planes_f], out_hbm.at[row, planes_f], out_sem.at[row, f])

    inner, edges = list(range(1, rows - 1)), [0, rows - 1]

    def arrived(sweep, f):
        @pl.when(north)
        def _():
            halo_copy(sweep, 1, f).wait_recv()

        @pl.when(south)
        def _():
            halo_copy(sweep, 0, f).wait_recv()

    def first_inner(f, carry):
        for row in inner:
            relax(first, second, row, f)
        return carry

    lax.fori_loop(0, FLD, first_inner, 0)

    def first_edges(f, carry):
        arrived(0, f)
        relax(first, second, 0, f)

        @pl.when(north)
        def _():
            halo_copy(1, 0, f).start()

        relax(first, second, rows - 1, f)

        @pl.when(south)
        def _():
            halo_copy(1, 1, f).start()

        return carry

    lax.fori_loop(0, FLD, first_edges, 0)

    def second_inner(f, carry):
        for row in inner:
            relax(second, departed, row, f)
            out_copy(row, f).start()
        return carry

    lax.fori_loop(0, FLD, second_inner, 0)

    def second_edges(f, carry):
        arrived(1, f)
        for row in edges:
            relax(second, departed, row, f)
            out_copy(row, f).start()
        return carry

    lax.fori_loop(0, FLD, second_edges, 0)

    for r in others:

        @pl.when(there(r))
        def _():
            list_copy(r).wait_send()
            block_copy(r).wait_send()

    def finish(f, carry):
        for sweep in range(SWEEPS):

            @pl.when(north)
            def _():
                halo_copy(sweep, 0, f).wait_send()

            @pl.when(south)
            def _():
                halo_copy(sweep, 1, f).wait_send()

        for row in range(rows):
            out_copy(row, f).wait()
        return carry

    lax.fori_loop(0, FLD, finish, 0)


def per_device(bands, fields, helm_coef, weight_table, fetch_list, source_owner, source_slot, weight_index):
    rows, nblocks, planes, width = fields.shape
    offsets, cap = fetch_list.shape[1:]
    reach = (offsets - 1) // 2
    lon = nblocks * width
    position = lax.axis_index("lat")
    lists = fetch_list[0]
    pool_index = (source_owner - position + reach) * cap + source_slot
    vmem = pl.BlockSpec(memory_space=pltpu.VMEM)
    smem = pl.BlockSpec(memory_space=pltpu.SMEM)
    anywhere = pl.BlockSpec(memory_space=pl.ANY)
    dma = pltpu.SemaphoreType.DMA
    result = pl.pallas_call(
        functools.partial(relax_kernel, reach, bands),
        out_shape=jax.ShapeDtypeStruct((rows, planes, lon), jnp.float32),
        in_specs=[vmem, smem, vmem, vmem, anywhere, anywhere, anywhere],
        out_specs=anywhere,
        scratch_shapes=[
            pltpu.VMEM(weight_table.shape, weight_table.dtype),
            pltpu.SMEM(pool_index.shape, jnp.int32),
            pltpu.SMEM(weight_index.shape, jnp.int32),
            pltpu.VMEM((offsets, offsets, cap), jnp.int32),
            pltpu.SMEM((offsets, offsets, cap), jnp.int32),
            pltpu.VMEM((offsets, cap, planes, width), fields.dtype),
            pltpu.VMEM((offsets * cap, planes, width), fields.dtype),
            pltpu.VMEM((rows, lon), jnp.float32),
            pltpu.VMEM((rows, planes, lon), jnp.float32),
            pltpu.VMEM((rows + 2, planes, lon), jnp.float32),
            pltpu.VMEM((rows + 2, planes, lon), jnp.float32),
            dma((3,)),
            dma((offsets,)),
            dma((offsets,)),
            dma((offsets,)),
            dma((offsets,)),
            dma((offsets,)),
            dma((SWEEPS, 2, FLD)),
            dma((SWEEPS, 2, FLD)),
            dma((rows, FLD)),
        ],
        compiler_params=pltpu.CompilerParams(
            collective_id=0, has_side_effects=True, vmem_limit_bytes=56 * 1024 * 1024
        ),
        cost_estimate=pl.CostEstimate(
            flops=2 * source_owner.size * planes * width * width,
            bytes_accessed=fields.size * 2 + weight_table.size * 2 + rows * planes * lon * 4,
            transcendentals=0,
        ),
    )(fields.reshape(rows * nblocks, planes, width), lists, lists, helm_coef, weight_table, pool_index, weight_index)
    return result.reshape(rows, FLD, LEV, lon)


def solution(mesh):
    return jax.shard_map(
        functools.partial(per_device, mesh.shape["lat"]),
        mesh=mesh,
        in_specs=(
            P(("group", "lat"), None, None, None),
            P("lat", None),
            P(),
            P(("group", "lat"), None, None),
            P(("group", "lat"), None, None),
            P(("group", "lat"), None, None),
            P(("group", "lat"), None, None),
        ),
        out_specs=P(("group", "lat"), None, None, None),
        check_vma=False,
    )
```

```python
import functools

import jax
import jax.numpy as jnp
from jax import lax
from jax.experimental import pallas as pl
from jax.experimental.pallas import tpu as pltpu
from jax.sharding import PartitionSpec as P

FLD = 4
LEV = 16
SWEEPS = 2

lon_coupling = 0.25
lat_coupling = 1.0
lev_coupling = 0.25

MESH = pl.DeviceIdType.MESH


def relax_kernel(
    reach,
    bands,
    fields_ref,
    lists_smem,
    lists_vmem,
    helm_ref,
    owner_ref,
    slot_ref,
    table_hbm,
    weight_index_hbm,
    out_hbm,
    table,
    pool_vmem,
    pool_index,
    weight_index,
    asked_vmem,
    asked,
    packed,
    pool,
    inverse,
    departed,
    first,
    second,
    near_out,
    near_in,
    code_out,
    code_in,
    step_out,
    step_in,
    local_sem,
    list_send,
    list_recv,
    asked_sem,
    block_send,
    block_recv,
    halo_send,
    halo_recv,
    out_sem,
):
    me = lax.axis_index("lat")
    offsets, _, cap = lists_smem.shape
    rows, planes, lon = departed.shape
    width = fields_ref.shape[2]
    nblocks = lon // width
    taps = pool_index.shape[1]
    others = [r for r in range(offsets) if r != reach]
    others.sort(key=lambda r: -abs(r - reach))

    def there(step):
        band = me + (step - reach)
        return (band >= 0) & (band < bands)

    barrier = pltpu.get_barrier_semaphore()
    count = jnp.int32(0)
    for r in others:

        @pl.when(there(r))
        def _():
            pl.semaphore_signal(barrier, inc=1, device_id={"lat": me + (r - reach)}, device_id_type=MESH)

        count = count + there(r).astype(jnp.int32)
    pl.semaphore_wait(barrier, count)

    def list_copy(r):
        back = 2 * reach - r
        return pltpu.make_async_remote_copy(
            src_ref=lists_vmem,
            dst_ref=asked_vmem.at[back],
            send_sem=list_send.at[r],
            recv_sem=list_recv.at[back],
            device_id={"lat": me + (r - reach)},
            device_id_type=MESH,
        )

    for r in others:

        @pl.when(there(r))
        def _():
            list_copy(r).start()

    place = (owner_ref[...] - me + reach) * cap + slot_ref[...]
    pool_vmem[...] = jnp.clip(place, 0, offsets * cap - 1)
    locals_ = [
        pltpu.make_async_copy(table_hbm, table, local_sem.at[0]),
        pltpu.make_async_copy(pool_vmem, pool_index, local_sem.at[1]),
        pltpu.make_async_copy(weight_index_hbm, weight_index, local_sem.at[2]),
    ]
    for copy in locals_:
        copy.start()

    def asked_copy(r):
        return pltpu.make_async_copy(asked_vmem.at[r], asked.at[r], asked_sem.at[r])

    for r in others:

        @pl.when(there(r))
        def _():
            list_copy(2 * reach - r).wait_recv()
            asked_copy(r).start()

    def block_copy(r):
        back = 2 * reach - r
        return pltpu.make_async_remote_copy(
            src_ref=packed.at[r],
            dst_ref=pool.at[pl.ds(back * cap, cap)],
            send_sem=block_send.at[r],
            recv_sem=block_recv.at[back],
            device_id={"lat": me + (r - reach)},
            device_id_type=MESH,
        )

    unroll = 8 if cap % 8 == 0 else 1
    for r in others:

        @pl.when(there(r))
        def _():
            asked_copy(r).wait()

            def pack(j, carry):
                for u in range(unroll):
                    packed[r, j * unroll + u] = fields_ref[asked[r, 2 * reach - r, 0, j * unroll + u]]
                return carry

            lax.fori_loop(0, cap // unroll, pack, 0)
            block_copy(r).start()

    def pack_own(j, carry):
        for u in range(unroll):
            pool[reach * cap + j * unroll + u] = fields_ref[lists_smem[reach, 0, j * unroll + u]]
        return carry

    lax.fori_loop(0, cap // unroll, pack_own, 0)

    total_coupling = 2.0 * (lon_coupling + lat_coupling + lev_coupling)
    inverse[...] = 1.0 / (helm_ref[...] + total_coupling)

    for side, alone in ((0, me == 0), (1, me == bands - 1)):

        @pl.when(alone)
        def _():
            near_in[side] = jnp.zeros((planes, lon), near_in.dtype)
            code_in[side] = jnp.zeros((planes, lon), code_in.dtype)
            step_in[side] = jnp.zeros((FLD, 1, lon), jnp.float32)

    for copy in locals_:
        copy.wait()
    for r in others:

        @pl.when(there(r))
        def _():
            block_copy(2 * reach - r).wait_recv()

    north, south = me > 0, me < bands - 1

    def halo_copy(kind, way, f):
        planes_f = pl.ds(pl.multiple_of(f * LEV, LEV), LEV)
        sent = (near_out, code_out, step_out)[kind]
        landed = (near_in, code_in, step_in)[kind]
        part = f if kind == 2 else planes_f
        return pltpu.make_async_remote_copy(
            src_ref=sent.at[way, part],
            dst_ref=landed.at[1 - way, part],
            send_sem=halo_send.at[kind, way, f],
            recv_sem=halo_recv.at[kind, way, f],
            device_id={"lat": me - 1 if way == 0 else me + 1},
            device_id_type=MESH,
        )

    def interpolate(row):
        def one_block(b):
            columns = pl.ds(pl.multiple_of(b * width, width), width)
            sources = jnp.concatenate([pool[pool_index[row, t, b]] for t in range(taps)], axis=1)
            weights = jnp.concatenate([table[weight_index[row, t, b]] for t in range(taps)], axis=0)
            value = jnp.dot(sources, weights, preferred_element_type=jnp.float32)
            departed[row, :, columns] = value
            start = value * inverse[row : row + 1, columns]
            first[row, :, columns] = start
            if row == 0:
                near_out[0, :, columns] = start.astype(near_out.dtype)
            if row == rows - 1:
                near_out[1, :, columns] = start.astype(near_out.dtype)

        pair = 2 if nblocks % 2 == 0 else 1

        def some_blocks(b, carry):
            for u in range(pair):
                one_block(b * pair + u)
            return carry

        lax.fori_loop(0, nblocks // pair, some_blocks, 0)

    order = [0, rows - 1] + list(range(1, rows - 1))
    for row in order:
        interpolate(row)
        if row == 0:

            @pl.when(north)
            def _():
                for f in range(FLD):
                    halo_copy(0, 0, f).start()

        if row == rows - 1:

            @pl.when(south)
            def _():
                for f in range(FLD):
                    halo_copy(0, 1, f).start()

    chunk = 1024 if lon % 1024 == 0 else width
    lane = 128

    def row_of(held, row, f, planes_f, here):
        if 0 <= row < rows:
            return held[row, planes_f, here]
        side = 0 if row < 0 else 1
        if held is first:
            return near_in[side, planes_f, here].astype(jnp.float32)
        codes = code_in[side, planes_f, here].astype(jnp.int32).astype(jnp.float32)
        return codes * step_in[side, f, :, here]

    def encode(value, way, f, planes_f, here):
        largest = jnp.maximum(jnp.max(jnp.abs(value), axis=0, keepdims=True), 1e-30)
        codes = jnp.floor(value * (32767.0 / largest) + 0.5)
        code_out[way, planes_f, here] = codes.astype(jnp.int32).astype(jnp.int16)
        step_out[way, f, :, here] = largest * (1.0 / 32767.0)

    def relax(held, result, row, f):
        planes_f = pl.ds(pl.multiple_of(f * LEV, LEV), LEV)
        for start in range(0, lon, chunk):
            here = pl.ds(start, chunk)
            mid = held[row, planes_f, here]
            west = held[row, planes_f, pl.ds((start - lane) % lon, lane)]
            east = held[row, planes_f, pl.ds((start + chunk) % lon, lane)]
            wide = jnp.concatenate([west, mid, east], axis=1)
            span = chunk + 2 * lane
            beside = pltpu.roll(wide, 1, 1) + pltpu.roll(wide, span - 1, 1)
            beside = beside[:, lane : lane + chunk]
            level = lax.broadcasted_iota(jnp.int32, (LEV, chunk), 0)
            above = jnp.where(level > 0, pltpu.roll(mid, 1, 0), 0.0)
            below = jnp.where(level < LEV - 1, pltpu.roll(mid, LEV - 1, 0), 0.0)
            across = row_of(held, row - 1, f, planes_f, here) + row_of(held, row + 1, f, planes_f, here)
            coupled = lon_coupling * beside + lat_coupling * across + lev_coupling * (above + below)
            value = (departed[row, planes_f, here] + coupled) * inverse[row : row + 1, here]
            result[row, planes_f, here] = value
            if held is first and row == 0:
                encode(value, 0, f, planes_f, here)
            if held is first and row == rows - 1:
                encode(value, 1, f, planes_f, here)

    def out_copy(row, f):
        planes_f = pl.ds(pl.multiple_of(f * LEV, LEV), LEV)
        return pltpu.make_async_copy(departed.at[row, planes_f], out_hbm.at[row, planes_f], out_sem.at[row, f])

    inner, edges = list(range(1, rows - 1)), [0, rows - 1]

    kinds = ((0,), (1, 2))

    def arrived(sweep, f):
        @pl.when(north)
        def _():
            for kind in kinds[sweep]:
                halo_copy(kind, 1, f).wait_recv()

        @pl.when(south)
        def _():
            for kind in kinds[sweep]:
                halo_copy(kind, 0, f).wait_recv()

    def first_inner(f, carry):
        for row in inner:
            relax(first, second, row, f)
        return carry

    lax.fori_loop(0, FLD, first_inner, 0)

    def first_edges(f, carry):
        arrived(0, f)
        relax(first, second, 0, f)

        @pl.when(north)
        def _():
            for kind in kinds[1]:
                halo_copy(kind, 0, f).start()

        relax(first, second, rows - 1, f)

        @pl.when(south)
        def _():
            for kind in kinds[1]:
                halo_copy(kind, 1, f).start()

        return carry

    lax.fori_loop(0, FLD, first_edges, 0)

    def second_inner(f, carry):
        for row in inner:
            relax(second, departed, row, f)
            out_copy(row, f).start()
        return carry

    lax.fori_loop(0, FLD, second_inner, 0)

    def second_edges(f, carry):
        arrived(1, f)
        for row in edges:
            relax(second, departed, row, f)
            out_copy(row, f).start()
        return carry

    lax.fori_loop(0, FLD, second_edges, 0)

    for r in others:

        @pl.when(there(r))
        def _():
            list_copy(r).wait_send()
            block_copy(r).wait_send()

    def finish(f, carry):
        for kind in range(3):

            @pl.when(north)
            def _():
                halo_copy(kind, 0, f).wait_send()

            @pl.when(south)
            def _():
                halo_copy(kind, 1, f).wait_send()

        for row in range(rows):
            out_copy(row, f).wait()
        return carry

    lax.fori_loop(0, FLD, finish, 0)


def per_device(bands, fields, helm_coef, weight_table, fetch_list, source_owner, source_slot, weight_index):
    rows, nblocks, planes, width = fields.shape
    offsets, cap = fetch_list.shape[1:]
    reach = (offsets - 1) // 2
    lon = nblocks * width
    taps = source_owner.shape[2]
    lists = fetch_list.transpose(1, 0, 2)
    owner, slot, weight = (x.transpose(0, 2, 1) for x in (source_owner, source_slot, weight_index))
    vmem = pl.BlockSpec(memory_space=pltpu.VMEM)
    smem = pl.BlockSpec(memory_space=pltpu.SMEM)
    anywhere = pl.BlockSpec(memory_space=pl.ANY)
    dma = pltpu.SemaphoreType.DMA
    result = pl.pallas_call(
        functools.partial(relax_kernel, reach, bands),
        out_shape=jax.ShapeDtypeStruct((rows, planes, lon), jnp.float32),
        in_specs=[vmem, smem, vmem, vmem, vmem, vmem, anywhere, anywhere],
        out_specs=anywhere,
        scratch_shapes=[
            pltpu.VMEM(weight_table.shape, weight_table.dtype),
            pltpu.VMEM((rows, taps, nblocks), jnp.int32),
            pltpu.SMEM((rows, taps, nblocks), jnp.int32),
            pltpu.SMEM((rows, taps, nblocks), jnp.int32),
            pltpu.VMEM((offsets, offsets, 1, cap), jnp.int32),
            pltpu.SMEM((offsets, offsets, 1, cap), jnp.int32),
            pltpu.VMEM((offsets, cap, planes, width), fields.dtype),
            pltpu.VMEM((offsets * cap, planes, width), fields.dtype),
            pltpu.VMEM((rows, lon), jnp.float32),
            pltpu.VMEM((rows, planes, lon), jnp.float32),
            pltpu.VMEM((rows, planes, lon), jnp.float32),
            pltpu.VMEM((rows, planes, lon), jnp.float32),
            pltpu.VMEM((2, planes, lon), jnp.bfloat16),
            pltpu.VMEM((2, planes, lon), jnp.bfloat16),
            pltpu.VMEM((2, planes, lon), jnp.int16),
            pltpu.VMEM((2, planes, lon), jnp.int16),
            pltpu.VMEM((2, FLD, 1, lon), jnp.float32),
            pltpu.VMEM((2, FLD, 1, lon), jnp.float32),
            dma((3,)),
            dma((offsets,)),
            dma((offsets,)),
            dma((offsets,)),
            dma((offsets,)),
            dma((offsets,)),
            dma((3, 2, FLD)),
            dma((3, 2, FLD)),
            dma((rows, FLD)),
        ],
        compiler_params=pltpu.CompilerParams(
            collective_id=0, has_side_effects=True, vmem_limit_bytes=46 * 1024 * 1024
        ),
        cost_estimate=pl.CostEstimate(
            flops=2 * source_owner.size * planes * width * width,
            bytes_accessed=fields.size * 2 + weight_table.size * 2 + rows * planes * lon * 4,
            transcendentals=0,
        ),
    )(fields.reshape(rows * nblocks, planes, width), lists, lists, helm_coef, owner, slot, weight_table, weight)
    return result.reshape(rows, FLD, LEV, lon)


def solution(mesh):
    return jax.shard_map(
        functools.partial(per_device, mesh.shape["lat"]),
        mesh=mesh,
        in_specs=(
            P(("group", "lat"), None, None, None),
            P("lat", None),
            P(),
            P(("group", "lat"), None, None),
            P(("group", "lat"), None, None),
            P(("group", "lat"), None, None),
            P(("group", "lat"), None, None),
        ),
        out_specs=P(("group", "lat"), None, None, None),
        check_vma=False,
    )
```

```python
import functools

import jax
import jax.numpy as jnp
from jax import lax
from jax.experimental import pallas as pl
from jax.experimental.pallas import tpu as pltpu
from jax.sharding import PartitionSpec as P

FLD = 4
LEV = 16
SWEEPS = 2

lon_coupling = 0.25
lat_coupling = 1.0
lev_coupling = 0.25

MESH = pl.DeviceIdType.MESH


def relax_kernel(
    reach,
    bands,
    fields_hbm,
    lists_hbm,
    helm_hbm,
    owner_hbm,
    slot_hbm,
    table_hbm,
    weight_index_hbm,
    out_hbm,
    fields_ref,
    lists_smem,
    owner_ref,
    slot_ref,
    table,
    pool_vmem,
    pool_index,
    weight_index,
    asked_vmem,
    asked,
    packed,
    pool,
    inverse,
    departed,
    first,
    second,
    near_out,
    near_in,
    code_out,
    code_in,
    step_out,
    step_in,
    local_sem,
    list_send,
    list_recv,
    asked_sem,
    block_send,
    block_recv,
    halo_send,
    halo_recv,
    out_sem,
):
    me = lax.axis_index("lat")
    offsets, _, cap = lists_smem.shape
    rows, planes, lon = departed.shape
    width = fields_ref.shape[2]
    nblocks = lon // width
    taps = pool_index.shape[1]
    others = [r for r in range(offsets) if r != reach]
    others.sort(key=lambda r: -abs(r - reach))

    def there(step):
        band = me + (step - reach)
        return (band >= 0) & (band < bands)

    brought = (
        (fields_hbm, fields_ref),
        (owner_hbm, owner_ref),
        (slot_hbm, slot_ref),
        (lists_hbm, lists_smem),
        (weight_index_hbm, weight_index),
        (helm_hbm, inverse),
        (table_hbm, table),
    )
    locals_ = [pltpu.make_async_copy(a, b, local_sem.at[k]) for k, (a, b) in enumerate(brought)]
    for copy in locals_:
        copy.start()

    barrier = pltpu.get_barrier_semaphore()
    count = jnp.int32(0)
    for r in others:

        @pl.when(there(r))
        def _():
            pl.semaphore_signal(barrier, inc=1, device_id={"lat": me + (r - reach)}, device_id_type=MESH)

        count = count + there(r).astype(jnp.int32)
    pl.semaphore_wait(barrier, count)

    def list_copy(r):
        back = 2 * reach - r
        return pltpu.make_async_remote_copy(
            src_ref=lists_hbm,
            dst_ref=asked_vmem.at[back],
            send_sem=list_send.at[r],
            recv_sem=list_recv.at[back],
            device_id={"lat": me + (r - reach)},
            device_id_type=MESH,
        )

    for r in others:

        @pl.when(there(r))
        def _():
            list_copy(r).start()

    locals_[1].wait()
    locals_[2].wait()
    place = (owner_ref[...] - me + reach) * cap + slot_ref[...]
    pool_vmem[...] = jnp.clip(place, 0, offsets * cap - 1)
    pool_copy = pltpu.make_async_copy(pool_vmem, pool_index, local_sem.at[len(brought)])
    pool_copy.start()

    def asked_copy(r):
        return pltpu.make_async_copy(asked_vmem.at[r], asked.at[r], asked_sem.at[r])

    for r in others:

        @pl.when(there(r))
        def _():
            list_copy(2 * reach - r).wait_recv()
            asked_copy(r).start()

    locals_[0].wait()

    def block_copy(r):
        back = 2 * reach - r
        return pltpu.make_async_remote_copy(
            src_ref=packed.at[r],
            dst_ref=pool.at[pl.ds(back * cap, cap)],
            send_sem=block_send.at[r],
            recv_sem=block_recv.at[back],
            device_id={"lat": me + (r - reach)},
            device_id_type=MESH,
        )

    unroll = 8 if cap % 8 == 0 else 1
    for r in others:

        @pl.when(there(r))
        def _():
            asked_copy(r).wait()

            def pack(j, carry):
                for u in range(unroll):
                    packed[r, j * unroll + u] = fields_ref[asked[r, 2 * reach - r, 0, j * unroll + u]]
                return carry

            lax.fori_loop(0, cap // unroll, pack, 0)
            block_copy(r).start()

    for copy in locals_[3:]:
        copy.wait()
    pool_copy.wait()

    def pack_own(j, carry):
        for u in range(unroll):
            pool[reach * cap + j * unroll + u] = fields_ref[lists_smem[reach, 0, j * unroll + u]]
        return carry

    lax.fori_loop(0, cap // unroll, pack_own, 0)

    total_coupling = 2.0 * (lon_coupling + lat_coupling + lev_coupling)
    inverse[...] = 1.0 / (inverse[...] + total_coupling)

    for side, alone in ((0, me == 0), (1, me == bands - 1)):

        @pl.when(alone)
        def _():
            near_in[side] = jnp.zeros((planes, lon), near_in.dtype)
            code_in[side] = jnp.zeros((planes, lon), code_in.dtype)
            step_in[side] = jnp.zeros((FLD, 1, lon), jnp.float32)

    for r in others:

        @pl.when(there(r))
        def _():
            block_copy(2 * reach - r).wait_recv()

    north, south = me > 0, me < bands - 1

    def halo_copy(kind, way, f):
        planes_f = pl.ds(pl.multiple_of(f * LEV, LEV), LEV)
        sent = (near_out, code_out, step_out)[kind]
        landed = (near_in, code_in, step_in)[kind]
        part = f if kind == 2 else planes_f
        return pltpu.make_async_remote_copy(
            src_ref=sent.at[way, part],
            dst_ref=landed.at[1 - way, part],
            send_sem=halo_send.at[kind, way, f],
            recv_sem=halo_recv.at[kind, way, f],
            device_id={"lat": me - 1 if way == 0 else me + 1},
            device_id_type=MESH,
        )

    def interpolate(row):
        def one_block(b):
            columns = pl.ds(pl.multiple_of(b * width, width), width)
            sources = jnp.concatenate([pool[pool_index[row, t, b]] for t in range(taps)], axis=1)
            weights = jnp.concatenate([table[weight_index[row, t, b]] for t in range(taps)], axis=0)
            value = jnp.dot(sources, weights, preferred_element_type=jnp.float32)
            departed[row, :, columns] = value
            start = value * inverse[row : row + 1, columns]
            first[row, :, columns] = start
            if row == 0:
                near_out[0, :, columns] = start.astype(near_out.dtype)
            if row == rows - 1:
                near_out[1, :, columns] = start.astype(near_out.dtype)

        pair = 2 if nblocks % 2 == 0 else 1

        def some_blocks(b, carry):
            for u in range(pair):
                one_block(b * pair + u)
            return carry

        lax.fori_loop(0, nblocks // pair, some_blocks, 0)

    order = [0, rows - 1] + list(range(1, rows - 1))
    for row in order:
        interpolate(row)
        if row == 0:

            @pl.when(north)
            def _():
                for f in range(FLD):
                    halo_copy(0, 0, f).start()

        if row == rows - 1:

            @pl.when(south)
            def _():
                for f in range(FLD):
                    halo_copy(0, 1, f).start()

    chunk = 1024 if lon % 1024 == 0 else width
    lane = 128

    def row_of(held, row, f, planes_f, here):
        if 0 <= row < rows:
            return held[row, planes_f, here]
        side = 0 if row < 0 else 1
        if held is first:
            return near_in[side, planes_f, here].astype(jnp.float32)
        codes = code_in[side, planes_f, here].astype(jnp.int32).astype(jnp.float32)
        return codes * step_in[side, f, :, here]

    def encode(value, way, f, planes_f, here):
        largest = jnp.maximum(jnp.max(jnp.abs(value), axis=0, keepdims=True), 1e-30)
        codes = jnp.floor(value * (32767.0 / largest) + 0.5)
        code_out[way, planes_f, here] = codes.astype(jnp.int32).astype(jnp.int16)
        step_out[way, f, :, here] = largest * (1.0 / 32767.0)

    def relax(held, result, row, f):
        planes_f = pl.ds(pl.multiple_of(f * LEV, LEV), LEV)
        for start in range(0, lon, chunk):
            here = pl.ds(start, chunk)
            mid = held[row, planes_f, here]
            west = held[row, planes_f, pl.ds((start - lane) % lon, lane)]
            east = held[row, planes_f, pl.ds((start + chunk) % lon, lane)]
            wide = jnp.concatenate([west, mid, east], axis=1)
            span = chunk + 2 * lane
            beside = pltpu.roll(wide, 1, 1) + pltpu.roll(wide, span - 1, 1)
            beside = beside[:, lane : lane + chunk]
            level = lax.broadcasted_iota(jnp.int32, (LEV, chunk), 0)
            above = jnp.where(level > 0, pltpu.roll(mid, 1, 0), 0.0)
            below = jnp.where(level < LEV - 1, pltpu.roll(mid, LEV - 1, 0), 0.0)
            across = row_of(held, row - 1, f, planes_f, here) + row_of(held, row + 1, f, planes_f, here)
            coupled = lon_coupling * beside + lat_coupling * across + lev_coupling * (above + below)
            value = (departed[row, planes_f, here] + coupled) * inverse[row : row + 1, here]
            result[row, planes_f, here] = value
            if held is first and row == 0:
                encode(value, 0, f, planes_f, here)
            if held is first and row == rows - 1:
                encode(value, 1, f, planes_f, here)

    def out_copy(row, f):
        planes_f = pl.ds(pl.multiple_of(f * LEV, LEV), LEV)
        return pltpu.make_async_copy(departed.at[row, planes_f], out_hbm.at[row, planes_f], out_sem.at[row, f])

    inner, edges = list(range(1, rows - 1)), [0, rows - 1]

    kinds = ((0,), (1, 2))

    def arrived(sweep, f):
        @pl.when(north)
        def _():
            for kind in kinds[sweep]:
                halo_copy(kind, 1, f).wait_recv()

        @pl.when(south)
        def _():
            for kind in kinds[sweep]:
                halo_copy(kind, 0, f).wait_recv()

    def first_edges(f, carry):
        arrived(0, f)
        relax(first, second, 0, f)

        @pl.when(north)
        def _():
            for kind in kinds[1]:
                halo_copy(kind, 0, f).start()

        relax(first, second, rows - 1, f)

        @pl.when(south)
        def _():
            for kind in kinds[1]:
                halo_copy(kind, 1, f).start()

        for row in inner:
            relax(first, second, row, f)
        return carry

    lax.fori_loop(0, FLD, first_edges, 0)

    def second_inner(f, carry):
        for row in inner:
            relax(second, departed, row, f)
            out_copy(row, f).start()
        return carry

    lax.fori_loop(0, FLD, second_inner, 0)

    def second_edges(f, carry):
        arrived(1, f)
        for row in edges:
            relax(second, departed, row, f)
            out_copy(row, f).start()
        return carry

    lax.fori_loop(0, FLD, second_edges, 0)

    for r in others:

        @pl.when(there(r))
        def _():
            list_copy(r).wait_send()
            block_copy(r).wait_send()

    def finish(f, carry):
        for kind in range(3):

            @pl.when(north)
            def _():
                halo_copy(kind, 0, f).wait_send()

            @pl.when(south)
            def _():
                halo_copy(kind, 1, f).wait_send()

        for row in range(rows):
            out_copy(row, f).wait()
        return carry

    lax.fori_loop(0, FLD, finish, 0)


def per_device(bands, fields, helm_coef, weight_table, fetch_list, source_owner, source_slot, weight_index):
    rows, nblocks, planes, width = fields.shape
    offsets, cap = fetch_list.shape[1:]
    reach = (offsets - 1) // 2
    lon = nblocks * width
    taps = source_owner.shape[2]
    lists = fetch_list.transpose(1, 0, 2)
    owner, slot, weight = (x.transpose(0, 2, 1) for x in (source_owner, source_slot, weight_index))
    anywhere = pl.BlockSpec(memory_space=pl.ANY)
    dma = pltpu.SemaphoreType.DMA
    result = pl.pallas_call(
        functools.partial(relax_kernel, reach, bands),
        out_shape=jax.ShapeDtypeStruct((rows, planes, lon), jnp.float32),
        in_specs=[anywhere] * 7,
        out_specs=anywhere,
        scratch_shapes=[
            pltpu.VMEM((rows * nblocks, planes, width), fields.dtype),
            pltpu.SMEM((offsets, 1, cap), jnp.int32),
            pltpu.VMEM((rows, taps, nblocks), jnp.int32),
            pltpu.VMEM((rows, taps, nblocks), jnp.int32),
            pltpu.VMEM(weight_table.shape, weight_table.dtype),
            pltpu.VMEM((rows, taps, nblocks), jnp.int32),
            pltpu.SMEM((rows, taps, nblocks), jnp.int32),
            pltpu.SMEM((rows, taps, nblocks), jnp.int32),
            pltpu.VMEM((offsets, offsets, 1, cap), jnp.int32),
            pltpu.SMEM((offsets, offsets, 1, cap), jnp.int32),
            pltpu.VMEM((offsets, cap, planes, width), fields.dtype),
            pltpu.VMEM((offsets * cap, planes, width), fields.dtype),
            pltpu.VMEM((rows, lon), jnp.float32),
            pltpu.VMEM((rows, planes, lon), jnp.float32),
            pltpu.VMEM((rows, planes, lon), jnp.float32),
            pltpu.VMEM((rows, planes, lon), jnp.float32),
            pltpu.VMEM((2, planes, lon), jnp.bfloat16),
            pltpu.VMEM((2, planes, lon), jnp.bfloat16),
            pltpu.VMEM((2, planes, lon), jnp.int16),
            pltpu.VMEM((2, planes, lon), jnp.int16),
            pltpu.VMEM((2, FLD, 1, lon), jnp.float32),
            pltpu.VMEM((2, FLD, 1, lon), jnp.float32),
            dma((8,)),
            dma((offsets,)),
            dma((offsets,)),
            dma((offsets,)),
            dma((offsets,)),
            dma((offsets,)),
            dma((3, 2, FLD)),
            dma((3, 2, FLD)),
            dma((rows, FLD)),
        ],
        compiler_params=pltpu.CompilerParams(
            collective_id=0, has_side_effects=True, vmem_limit_bytes=58 * 1024 * 1024
        ),
        cost_estimate=pl.CostEstimate(
            flops=2 * source_owner.size * planes * width * width,
            bytes_accessed=fields.size * 2 + weight_table.size * 2 + rows * planes * lon * 4,
            transcendentals=0,
        ),
    )(fields.reshape(rows * nblocks, planes, width), lists, helm_coef, owner, slot, weight_table, weight)
    return result.reshape(rows, FLD, LEV, lon)


def solution(mesh):
    return jax.shard_map(
        functools.partial(per_device, mesh.shape["lat"]),
        mesh=mesh,
        in_specs=(
            P(("group", "lat"), None, None, None),
            P("lat", None),
            P(),
            P(("group", "lat"), None, None),
            P(("group", "lat"), None, None),
            P(("group", "lat"), None, None),
            P(("group", "lat"), None, None),
        ),
        out_specs=P(("group", "lat"), None, None, None),
        check_vma=False,
    )
```
